256 devices in a mesh: blk: 16 (over z, x_hi), group: 16 (over x_lo, y, core).
Axes of the slice: x: 4 (x_hi: 2, x_lo: 2; x = x_hi * 2 + x_lo), y: 4, z: 8, core: 2. Of those that a mesh axis runs over, the one named last changes fastest.
Arguments:
- images: float32 [262144, 1024], P(('blk', 'group')), may hold values from -0.1875 to 0.1875
- texts: float32 [2048, 1024], P(('blk', 'group')), may hold values from -0.1875 to 0.1875
- row_lse: float32 [262144], P(('blk', 'group')), may hold values from 12 to 14
- row_weights: float32 [262144], P(('blk', 'group')), may hold values from 0.3 to 3
- pair_ids: int32 [262144], P(('blk', 'group')), may hold values from 0 to 2047
Outputs:
- image_grads: float32 [262144, 1024], P(('blk', 'group'))
- text_grads: float32 [2048, 1024], P(('blk', 'group'))
The draws below stay inside these ranges and needn't reach their ends.
All inputs are finite; a program needn't handle non-finite values.
Results may differ from the reference program's by a relative error of at most 0.011.
Values may be sent and summed in bfloat16 or wider, within the bound.
A program may use at most 64 MiB of HBM per device.

```python
import math
import jax
import jax.numpy as jnp
from jax import lax

D = 1024
IMAGES = 262144
TEXTS = 2048


def embed_draw(key, rows):
    values = jnp.clip(jax.random.normal(key, (rows, D), jnp.float32), -6.0, 6.0)
    return values * (0.17320508 / jnp.sqrt(jnp.sqrt(jnp.float32(D))))


def draw_images(key, part):
    key = jax.random.fold_in(key, 11)
    return jnp.clip(embed_draw(key, IMAGES), -0.1875, 0.1875)


def draw_texts(key, part):
    key = jax.random.fold_in(key, 23)
    return jnp.clip(embed_draw(key, TEXTS), -0.1875, 0.1875)


def with_ends(result, rng, least, top_value):
    dims = result.shape
    place = [jax.random.randint(jax.random.fold_in(rng, axis), (), 0, dims[axis]) for axis in range(len(dims))]
    result = result.at[tuple(place)].set(least)
    longest = dims.index(max(dims))
    place[longest] = (place[longest] + 1) % dims[longest]
    return result.at[tuple(place)].set(top_value)


def level_of(own_key, extent, split, least, largest):
    factor_of, own = 1.0, jax.random.fold_in(own_key, 6)
    for position, shards_of in split:
        heights = jnp.exp(jax.random.uniform(jax.random.fold_in(own, position), (shards_of,), jnp.float32, least / len(split), largest / len(split)))
        factor_of = factor_of * jnp.repeat(heights, extent[position] // shards_of).reshape([-1 if axis == position else 1 for axis in range(len(extent))])
    return factor_of


def setup_inputs(seed: int = 0) -> dict:
    arg_keys = jax.random.split(jax.random.key(seed), 6)
    images = draw_images(jax.random.fold_in(arg_keys[5], 71), 0)
    texts = draw_texts(jax.random.fold_in(arg_keys[5], 71), 0)
    row_lse = jnp.clip(12.0 + 2.0 * jax.random.uniform(arg_keys[2], (IMAGES,), jnp.float32) ** level_of(arg_keys[2], (IMAGES,), ((0, 256),), -0.2, 0.2), 12.0, 14.0)
    row_weights = jnp.clip(jnp.exp(math.log(3.0) - 2.3025851 * jax.random.uniform(arg_keys[3], (IMAGES,), jnp.float32) ** level_of(arg_keys[3], (IMAGES,), ((0, 256),), -0.2, 0.2)), 0.3, 3.0)
    pair_ids = with_ends(jax.random.randint(arg_keys[4], (IMAGES,), 0, TEXTS), jax.random.fold_in(arg_keys[4], 1), 0, TEXTS - 1).astype(jnp.int32)
    return {"images": images, "texts": texts, "row_lse": row_lse, "row_weights": row_weights, "pair_ids": pair_ids}


logit_scale = 100.0


def reference(images, texts, row_lse, row_weights, pair_ids):
    image_low = lax.optimization_barrier(images.astype(jnp.bfloat16)).astype(jnp.float32)
    text_low = lax.optimization_barrier(texts.astype(jnp.bfloat16)).astype(jnp.float32)
    block = math.gcd(IMAGES, 4096)
    count = IMAGES // block
    columns = jnp.arange(TEXTS, dtype=jnp.int32)
    stacked = (image_low.reshape(count, block, D), row_lse.reshape(count, block),
               row_weights.reshape(count, block), pair_ids.reshape(count, block))

    def one_block(total, inputs):
        rows, lse, weights, ids = inputs
        scores = jnp.dot(rows, text_low.T, preferred_element_type=jnp.float32)
        match = (ids[:, None] == columns[None, :]).astype(jnp.float32)
        coeffs = weights[:, None] * (jnp.exp(logit_scale * scores - lse[:, None]) - match)
        coeffs = lax.optimization_barrier(coeffs.astype(jnp.bfloat16)).astype(jnp.float32)
        grads = logit_scale * jnp.dot(coeffs, text_low, preferred_element_type=jnp.float32)
        total = total + logit_scale * jnp.dot(coeffs.T, rows, preferred_element_type=jnp.float32)
        return total, grads

    text_grads, image_grads = lax.scan(one_block, jnp.zeros((TEXTS, D), jnp.float32), stacked)
    return image_grads.reshape(IMAGES, D), text_grads
```

```python
import jax
import jax.numpy as jnp
from jax import lax
from jax.sharding import PartitionSpec as P

logit_scale = 100.0


def shards(images, texts, row_lse, row_weights, pair_ids):
    image_low = images.astype(jnp.bfloat16)
    panel = lax.all_gather(texts.astype(jnp.bfloat16), ("blk", "group"), axis=0, tiled=True)
    columns = jnp.arange(panel.shape[0], dtype=jnp.int32)
    scores = jnp.einsum("rd,td->rt", image_low, panel, preferred_element_type=jnp.float32)
    match = (pair_ids[:, None] == columns[None, :]).astype(jnp.float32)
    coeffs = row_weights[:, None] * (jnp.exp(logit_scale * scores - row_lse[:, None]) - match)
    coeffs = coeffs.astype(jnp.bfloat16)
    terms = jnp.einsum("rt,rd->td", coeffs, image_low, preferred_element_type=jnp.float32)
    reduced = lax.psum_scatter(terms, ("blk", "group"), scatter_dimension=0, tiled=True)
    grads = logit_scale * jnp.dot(coeffs, panel, preferred_element_type=jnp.float32)
    return (grads, logit_scale * reduced)


def solution(mesh):
    placed = (
        P(("blk", "group"), None),
        P(("blk", "group"), None),
        P(("blk", "group")),
        P(("blk", "group")),
        P(("blk", "group")),
    )
    return jax.shard_map(
        shards,
        mesh=mesh,
        in_specs=placed,
        out_specs=(P(("blk", "group"), None), P(("blk", "group"), None)),
        check_vma=False,
    )
```

```python
import math

import jax
import jax.numpy as jnp
from jax import lax
from jax.experimental import pallas as pl
from jax.experimental.pallas import tpu as pltpu
from jax.sharding import PartitionSpec as P

logit_scale = 100.0
log2e = math.log2(math.e)

MESH = pl.DeviceIdType.MESH
BF, F32 = jnp.bfloat16, jnp.float32
NN = (((1,), (0,)), ((), ()))
NT = (((1,), (1,)), ((), ()))
TN = (((0,), (0,)), ((), ()))

NX, NY, NZ = 4, 4, 8
ROWS, D = 1024, 1024
TEXTS = 1024
GROUP = 256
HALF = D // 2


def device(x, y, z, c):
    return (z * 2 + x // 2, (x % 2) * 8 + y * 2 + c)


def dot(a, b, dims):
    return lax.dot_general(a, b, dims, preferred_element_type=F32)


def kernel(
    images, texts, lse, weights, ids, out_images, out_texts,
    stage, held, vec, blobs, panel, coeffs, own, sent, got, summed, got1, zsum, got2, igs, igr, outs,
    in_sem, out_sem, core_s, core_r, vec_s, vec_r, z_s, z_r, a_s, a_r, b_s, b_r, d_s, d_r,
    e_s, e_r, f_s, f_r, g_s, g_r, h_s, h_r,
):
    blk, group = lax.axis_index("blk"), lax.axis_index("group")
    z, x = blk // 2, (blk % 2) * 2 + group // 8
    y, c = (group // 2) % 4, group % 2
    last, first = (x, y), (y, x)

    def on_last(h, o):
        return device((x + o) % NX, y, z, c) if h == 0 else device(x, (y + o) % NY, z, c)

    def on_first(h, o):
        return on_last(1 - h, o)

    def on_z(o):
        return device(x, y, (z + o) % NZ, c)

    partner = device(x, y, z, 1 - c)

    barrier = pltpu.get_barrier_semaphore()
    peers = [partner] + [on_z(o) for o in range(1, NZ)]
    peers += [on_last(h, o) for h in range(2) for o in range(1, 4)]
    for peer in peers:
        pl.semaphore_signal(barrier, inc=1, device_id=peer, device_id_type=MESH)

    loads = []
    for k in range(4):
        rows = pl.ds(k * 256, 256)
        load = pltpu.make_async_copy(images.at[rows], stage.at[rows], in_sem.at[k])
        load.start()
        loads.append(load)

    sends = []

    def send(src, dst, ss, rs, peer):
        copy = pltpu.make_async_remote_copy(
            src_ref=src, dst_ref=dst, send_sem=ss, recv_sem=rs, device_id=peer, device_id_type=MESH
        )
        copy.start()
        sends.append(copy)
        return copy

    zh = z // 4
    za = x * (1 - zh) + y * zh
    zb = y * (1 - zh) + x * zh
    place = blobs.at[zh, za, zb, pl.ds(pl.multiple_of((z % 4) * 16, 16), 16)]
    t = texts[...]
    place[...] = jnp.concatenate([t[:, :HALF], t[:, HALF:]], axis=0).astype(BF)

    pl.semaphore_wait(barrier, len(peers))

    z_copies = [send(place, place, z_s.at[o - 1], z_r.at[o - 1], on_z(o)) for o in (1, 7, 2, 6, 3, 5, 4)]

    vec[0] = jnp.zeros((8, ROWS), F32)
    w = weights[...]
    vec[0, 0:1] = (jnp.log(w) - lse[...]) * log2e
    vec[0, 1:2] = ids[...].astype(F32)
    vec[0, 2:3] = w
    vec_copy = send(vec.at[0], vec.at[1], vec_s, vec_r, partner)

    core_copies = []
    for k in range(4):
        rows = pl.ds(k * 256, 256)
        loads[k].wait()
        held[rows] = stage[rows].astype(BF)
        core_copies.append(
            send(held.at[rows], held.at[pl.ds(ROWS + k * 256, 256)], core_s.at[k], core_r.at[k], partner)
        )

    for copy in z_copies:
        copy.wait_recv()

    a_copies = [[None] * 4 for _ in range(2)]
    b_copies = [[[None] * 4 for _ in range(2)] for _ in range(2)]

    def to_last(h, o):
        f = (first[h] - o + 4) % 4
        blob = blobs.at[h, last[h], f]
        for way, step in ((0, 1), (1, 3)):
            b_copies[h][way][o] = send(blob, blob, b_s.at[h, way, o], b_r.at[h, way, f], on_last(h, step))

    for h in range(2):
        blob = blobs.at[h, last[h], first[h]]
        for o in (1, 3, 2):
            a_copies[h][o] = send(blob, blob, a_s.at[h, o], a_r.at[h, o], on_first(h, o))
    for h in range(2):
        to_last(h, 0)
    for o in (1, 3, 2):
        for h in range(2):
            a_copies[h][o].wait_recv()
            to_last(h, o)

    def unpack(step, g):
        for h in range(2):
            a = (last[h] + step) % 4
            blob = blobs[h, a].reshape(GROUP, HALF).astype(F32).reshape(16, 2, 8, HALF)
            rows = pl.ds(g * GROUP + h * 128, 128)
            panel[rows, :HALF] = blob[:, 0].reshape(128, HALF).astype(BF)
            panel[rows, HALF:] = blob[:, 1].reshape(128, HALF).astype(BF)

    def scores(step, g):
        rows = pl.ds(g * GROUP, GROUP)
        r = lax.broadcasted_iota(jnp.int32, (GROUP, 1), 0)
        upper = r >= 128
        b = (r & 127) >> 5
        zz = ((r >> 7) << 2) + ((r & 31) >> 3)
        tx = jnp.where(upper, b, (x + step) % 4)
        ty = jnp.where(upper, (y + step) % 4, b)
        number = (zz * 256 + tx * 64 + ty * 16 + c * 8 + (r & 7)).astype(F32)

        for side in range(2):
            for k in range(4):
                lanes = slice(k * 256, (k + 1) * 256)
                cols = slice(side * ROWS + k * 256, side * ROWS + (k + 1) * 256)
                s = dot(panel[rows], held[cols], NT)
                e = jnp.exp2(s * (logit_scale * log2e) + vec[side, 0:1, lanes])
                e = e - jnp.where(number == vec[side, 1:2, lanes], vec[side, 2:3, lanes], 0.0)
                coeffs[rows, cols] = e.astype(BF)

    def terms(g, keep):
        rows = pl.ds(g * GROUP, GROUP)
        for j in range(2):
            lo = dot(coeffs[rows], held[:, j * 256 : (j + 1) * 256], NN)
            hi = dot(coeffs[rows], held[:, HALF + j * 256 : HALF + (j + 1) * 256], NN)
            both = jnp.stack([lo.reshape(32, 8, 256), hi.reshape(32, 8, 256)], axis=1).reshape(512, 256)
            keep(j, both)

    def keep_own(j, both):
        own[:, j * 256 : (j + 1) * 256] = both

    def keep_sent(g):
        def keep(j, both):
            sent[g - 1, :, j * 256 : (j + 1) * 256] = both.astype(BF)

        return keep

    for copy in core_copies:
        copy.wait_recv()
    vec_copy.wait_recv()

    unpack(0, 0)
    scores(0, 0)

    d_copies = [[None] * 4 for _ in range(2)]

    def arrived(h, way, f):
        a = (last[h] + (3 if way == 0 else 1)) % 4
        blob = blobs.at[h, a, f]
        return pltpu.make_async_remote_copy(
            src_ref=blob, dst_ref=blob, send_sem=b_s.at[h, way, 0], recv_sem=b_r.at[h, way, f],
            device_id=on_last(h, 1), device_id_type=MESH,
        ), blob

    for f in range(4):
        for h in range(2):
            way = 0 if f < 2 else 1
            copy, blob = arrived(h, way, f)
            copy.wait_recv()
            d_copies[h][f] = send(blob, blob, d_s.at[h, f], d_r.at[h, f], on_last(h, 1 if way == 0 else 3))
    for f in range(4):
        for h in range(2):
            copy, _ = arrived(h, 1 if f < 2 else 0, f)
            copy.wait_recv()

    e_copies = [[None] * 2 for _ in range(4)]
    for g, step in ((1, 3), (2, 1), (3, 2)):
        if g == 3:
            for h in range(2):
                for f in range(4):
                    d_copies[h][f].wait_recv()
        unpack(step, g)
        scores(step, g)
        terms(g, keep_sent(g))
        for h in range(2):
            half = pl.ds(h * 256, 256)
            e_copies[g][h] = send(
                sent.at[g - 1, half], got.at[g - 1, half], e_s.at[g - 1, h], e_r.at[g - 1, h], on_last(h, step)
            )
    terms(0, keep_own)

    f_copies = []

    def image_rows(k, base, keep):
        cols = slice(base + k * 256, base + (k + 1) * 256)
        for j in range(4):
            lanes = slice(j * 256, (j + 1) * 256)
            keep(k, lanes, dot(coeffs[:, cols], panel[:, lanes], TN))

    def keep_partner(k, lanes, grads):
        igs[k * 256 : (k + 1) * 256, lanes] = grads.astype(BF)

    def keep_mine(k, lanes, grads):
        rows = slice(k * 256, (k + 1) * 256)
        outs[rows, lanes] = (grads + igr[rows, lanes].astype(F32)).astype(BF)

    for k in range(4):
        image_rows(k, ROWS, keep_partner)
        rows = pl.ds(k * 256, 256)
        f_copies.append(send(igs.at[rows], igr.at[rows], f_s.at[k], f_r.at[k], partner))
    stores = []
    for k in range(4):
        rows = pl.ds(k * 256, 256)
        f_copies[k].wait_recv()
        image_rows(k, 0, keep_mine)
        store = pltpu.make_async_copy(outs.at[rows], out_images.at[rows], out_sem.at[k])
        store.start()
        stores.append(store)

    g_copies = []
    for h in range(2):
        half = pl.ds(h * 256, 256)
        total = own[half]
        for g in range(3):
            e_copies[g + 1][h].wait_recv()
            total = total + got[g, half].astype(F32)
        summed[half] = total.astype(BF)
        for o in (1, 3, 2):
            f = (first[h] + o) % 4
            rows = pl.ds(pl.multiple_of(h * 256 + f * 64, 64), 64)
            there = got1.at[o - 1, pl.ds(h * 64, 64)]
            g_copies.append(send(summed.at[rows], there, g_s.at[h, o - 1], g_r.at[h, o - 1], on_first(h, o)))
    for copy in g_copies:
        copy.wait_recv()
    for h in range(2):
        mine = summed[pl.ds(pl.multiple_of(h * 256 + first[h] * 64, 64), 64)].astype(F32)
        rows = pl.ds(h * 64, 64)
        for o in range(3):
            mine = mine + got1[o, rows].astype(F32)
        zsum[rows] = mine.astype(BF)
    h_copies = []
    for o in (1, 7, 2, 6, 3, 5, 4):
        rows = pl.ds(pl.multiple_of(((z + o) % NZ) * 16, 16), 16)
        h_copies.append(send(zsum.at[rows], got2.at[o - 1], h_s.at[o - 1], h_r.at[o - 1], on_z(o)))
    total = zsum[pl.ds(pl.multiple_of(z * 16, 16), 16)].astype(F32)
    for copy in h_copies:
        copy.wait_recv()
    for o in range(7):
        total = total + got2[o].astype(F32)
    total = total * logit_scale
    out_texts[:, :HALF] = total[:8]
    out_texts[:, HALF:] = total[8:]

    for copy in sends:
        copy.wait_send()
    for store in stores:
        store.wait()


def shards(images, texts, row_lse, row_weights, pair_ids):
    vm = pl.BlockSpec(memory_space=pltpu.VMEM)
    hbm = pl.BlockSpec(memory_space=pl.ANY)
    dma = pltpu.SemaphoreType.DMA
    grads, text_grads = pl.pallas_call(
        kernel,
        out_shape=(
            jax.ShapeDtypeStruct((ROWS, D), BF),
            jax.ShapeDtypeStruct((8, D), F32),
        ),
        in_specs=[hbm, vm, vm, vm, vm],
        out_specs=(hbm, vm),
        scratch_shapes=[
            pltpu.VMEM((ROWS, D), F32),
            pltpu.VMEM((2 * ROWS, D), BF),
            pltpu.VMEM((2, 8, ROWS), F32),
            pltpu.VMEM((2, 4, 4, 64, HALF), BF),
            pltpu.VMEM((TEXTS, D), BF),
            pltpu.VMEM((TEXTS, 2 * ROWS), BF),
            pltpu.VMEM((512, HALF), F32),
            pltpu.VMEM((3, 512, HALF), BF),
            pltpu.VMEM((3, 512, HALF), BF),
            pltpu.VMEM((512, HALF), BF),
            pltpu.VMEM((3, 128, HALF), BF),
            pltpu.VMEM((128, HALF), BF),
            pltpu.VMEM((7, 16, HALF), BF),
            pltpu.VMEM((ROWS, D), BF),
            pltpu.VMEM((ROWS, D), BF),
            pltpu.VMEM((ROWS, D), BF),
            dma((4,)), dma((4,)), dma((4,)), dma((4,)), dma, dma, dma((7,)), dma((7,)),
            dma((2, 4)), dma((2, 4)), dma((2, 2, 4)), dma((2, 2, 4)), dma((2, 4)), dma((2, 4)),
            dma((3, 2)), dma((3, 2)), dma((4,)), dma((4,)), dma((2, 3)), dma((2, 3)), dma((7,)), dma((7,)),
        ],
        compiler_params=pltpu.CompilerParams(
            collective_id=0, has_side_effects=True, vmem_limit_bytes=48 << 20
        ),
        name="tile",
    )(
        images, texts, row_lse.reshape(1, ROWS), row_weights.reshape(1, ROWS), pair_ids.reshape(1, ROWS)
    )
    return logit_scale * grads.astype(F32), text_grads


def solution(mesh):
    placed = (
        P(("blk", "group"), None),
        P(("blk", "group"), None),
        P(("blk", "group")),
        P(("blk", "group")),
        P(("blk", "group")),
    )
    return jax.shard_map(
        shards,
        mesh=mesh,
        in_specs=placed,
        out_specs=(P(("blk", "group"), None), P(("blk", "group"), None)),
        check_vma=False,
    )
```

```python
import math

import jax
import jax.numpy as jnp
from jax import lax
from jax.experimental import pallas as pl
from jax.experimental.pallas import tpu as pltpu
from jax.sharding import PartitionSpec as P

logit_scale = 100.0
log2e = math.log2(math.e)

MESH = pl.DeviceIdType.MESH
BF, F32 = jnp.bfloat16, jnp.float32
NN = (((1,), (0,)), ((), ()))
NT = (((1,), (1,)), ((), ()))
TN = (((0,), (0,)), ((), ()))

NX, NY, NZ = 4, 4, 8
ROWS, D = 1024, 1024
TEXTS = 1024
GROUP = 256
HALF = D // 2


def device(x, y, z, c):
    return (z * 2 + x // 2, (x % 2) * 8 + y * 2 + c)


def dot(a, b, dims):
    return lax.dot_general(a, b, dims, preferred_element_type=F32)


def kernel(
    images, texts, lse, weights, ids, out_images, out_texts,
    stage, texts_in, rows_in, ids_in, held, vec, blobs, panel, coeffs, sent, got, summed, done, got1, got2, mine, igs, igr,
    in_sem, row_sem, core_s, core_r, vec_s, vec_r, z_s, z_r, a_s, a_r, b_s, b_r, d_s, d_r,
    e_s, e_r, f_s, f_r, g_s, g_r, h_s, h_r,
):
    blk, group = lax.axis_index("blk"), lax.axis_index("group")
    z, x = blk // 2, (blk % 2) * 2 + group // 8
    y, c = (group // 2) % 4, group % 2
    zh = z // 4
    last, first = (x, y), (y, x)

    def on_last(h, o):
        return device((x + o) % NX, y, z, c) if h == 0 else device(x, (y + o) % NY, z, c)

    def on_first(h, o):
        return on_last(1 - h, o)

    def on_own_first(o):
        return device((x + o * zh) % NX, (y + o * (1 - zh)) % NY, z, c)

    def on_z(o):
        return device(x, y, (z + o) % NZ, c)

    partner = device(x, y, z, 1 - c)

    def load(src, dst, sem):
        copy = pltpu.make_async_copy(src, dst, sem)
        copy.start()
        return copy

    texts_load = load(texts, texts_in, row_sem.at[0])
    barrier = pltpu.get_barrier_semaphore()
    peers = [partner] + [on_z(o) for o in range(1, NZ)]
    peers += [on_last(h, o) for h in range(2) for o in range(1, 4)]
    for peer in peers:
        pl.semaphore_signal(barrier, inc=1, device_id=peer, device_id_type=MESH)

    loads = []
    for k in range(4):
        rows = pl.ds(k * 256, 256)
        loads.append(load(images.at[rows], stage.at[rows], in_sem.at[k]))
    row_loads = [
        load(lse, rows_in.at[pl.ds(0, 1)], row_sem.at[1]),
        load(weights, rows_in.at[pl.ds(1, 1)], row_sem.at[2]),
        load(ids, ids_in, row_sem.at[3]),
    ]

    sends = []

    def send(src, dst, ss, rs, peer):
        copy = pltpu.make_async_remote_copy(
            src_ref=src, dst_ref=dst, send_sem=ss, recv_sem=rs, device_id=peer, device_id_type=MESH
        )
        copy.start()
        sends.append(copy)
        return copy

    za = x * (1 - zh) + y * zh
    zb = y * (1 - zh) + x * zh
    place = blobs.at[zh, za, zb, pl.ds(pl.multiple_of((z % 4) * 16, 16), 16)]
    texts_load.wait()
    t = texts_in[...]
    place[...] = jnp.concatenate([t[:, :HALF], t[:, HALF:]], axis=0).astype(BF)

    pl.semaphore_wait(barrier, len(peers))

    z_copies = [send(place, place, z_s.at[o - 1], z_r.at[o - 1], on_z(o)) for o in (1, 7, 2, 6, 3, 5, 4)]

    vec[0] = jnp.zeros((8, ROWS), F32)
    for copy in row_loads:
        copy.wait()
    w = rows_in[1:2]
    vec[0, 0:1] = (jnp.log(w) - rows_in[0:1]) * log2e
    vec[0, 1:2] = ids_in[...].astype(F32)
    vec[0, 2:3] = w
    vec_copy = send(vec.at[0], vec.at[1], vec_s, vec_r, partner)

    for k in range(4):
        rows = pl.ds(k * 256, 256)
        loads[k].wait()
        held[rows] = stage[rows].astype(BF)

    for copy in z_copies:
        copy.wait_recv()

    a_copies, b_copies, d_copies = {}, {}, {}

    def place_of(h, o):
        return (first[h] - o + 4) % 4

    def to_last(h, o):
        blob = blobs.at[h, last[h], place_of(h, o)]
        for way, step in ((0, 1), (1, 3)):
            b_copies[h, way, o] = send(blob, blob, b_s.at[h, way, o], b_r.at[h, way, o], on_last(h, step))
        if o >= 2:
            d_copies[h, o] = send(blob, blob, d_s.at[h, o], d_r.at[h, o], on_last(h, 2))

    def relay(h, o):
        b_copies[h, o, o].wait_recv()
        blob = blobs.at[h, (last[h] + (3 if o == 0 else 1)) % 4, place_of(h, o)]
        d_copies[h, o] = send(blob, blob, d_s.at[h, o], d_r.at[h, o], on_last(h, 1 if o == 0 else 3))

    for h in range(2):
        blob = blobs.at[h, last[h], first[h]]
        for o in (1, 3, 2):
            a_copies[h, o] = send(blob, blob, a_s.at[h, o], a_r.at[h, o], on_first(h, o))
    for h in range(2):
        to_last(h, 0)
    core_copies = []
    for k in range(4):
        rows, there = pl.ds(k * 256, 256), pl.ds(ROWS + k * 256, 256)
        core_copies.append(send(held.at[rows], held.at[there], core_s.at[k], core_r.at[k], partner))
    for o in (1, 3, 2):
        for h in range(2):
            a_copies[h, o].wait_recv()
            to_last(h, o)
        if o == 1:
            for h in range(2):
                relay(h, 0)

    def unpack(o):
        for h in range(2):
            blob = blobs[h, :, place_of(h, o)].reshape(GROUP, HALF).astype(F32).reshape(16, 2, 8, HALF)
            rows = pl.ds(o * GROUP + h * 128, 128)
            panel[rows, :HALF] = blob[:, 0].reshape(128, HALF).astype(BF)
            panel[rows, HALF:] = blob[:, 1].reshape(128, HALF).astype(BF)

    def scores(o):
        rows = pl.ds(o * GROUP, GROUP)
        r = lax.broadcasted_iota(jnp.int32, (GROUP, 1), 0)
        a = (r & 127) >> 5
        zz = ((r >> 7) << 2) + ((r & 31) >> 3)
        chip = jnp.where(r >= 128, place_of(1, o) * 64 + a * 16, place_of(0, o) * 16 + a * 64)
        number = (zz * 256 + chip + c * 8 + (r & 7)).astype(F32)

        for side in range(2):
            for k in range(4):
                lanes = slice(k * 256, (k + 1) * 256)
                cols = slice(side * ROWS + k * 256, side * ROWS + (k + 1) * 256)
                s = dot(panel[rows], held[cols], NT)
                e = jnp.exp2(s * (logit_scale * log2e) + vec[side, 0:1, lanes])
                e = e - jnp.where(number == vec[side, 1:2, lanes], vec[side, 2:3, lanes], 0.0)
                coeffs[rows, cols] = e.astype(BF)

    def terms(o):
        rows = pl.ds(o * GROUP, GROUP)
        for j in range(2):
            lo = dot(coeffs[rows], held[:, j * 256 : (j + 1) * 256], NN)
            hi = dot(coeffs[rows], held[:, HALF + j * 256 : HALF + (j + 1) * 256], NN)
            both = jnp.stack([lo.reshape(32, 8, 256), hi.reshape(32, 8, 256)], axis=1).reshape(512, 256)
            sent[o, :, j * 256 : (j + 1) * 256] = both.astype(BF)

    def block(h, s):
        return pl.ds(pl.multiple_of(h * 256 + ((last[h] + s) % 4) * 64, 64), 64)

    for copy in core_copies:
        copy.wait_recv()
    vec_copy.wait_recv()

    e_copies = {}

    def give_terms(o):
        terms(o)
        for s in (2, 1, 3):
            for h in range(2):
                e_copies[h, o, s] = send(
                    sent.at[o, block(h, s)], got.at[o, h, s - 1],
                    e_s.at[o, h, s - 1], e_r.at[o, h, s - 1], on_last(h, s),
                )

    def over_last(h, o):
        total = sent[o, block(h, 0)].astype(F32)
        for s in (1, 3, 2):
            e_copies[h, o, s].wait_recv()
            total = total + got[o, h, s - 1].astype(F32)
        return total

    h_copies, g_copies = {}, {}

    def back_z(o):
        for h in range(2):
            summed[o, pl.ds(h * 64, 64)] = over_last(h, o).astype(BF)
        for d in (1, 7, 2, 6, 3, 5, 4):
            rows = pl.ds(pl.multiple_of(((z + d) % NZ) * 16, 16), 16)
            h_copies[o, d] = send(
                summed.at[o, rows], got2.at[o, d - 1], h_s.at[o, d - 1], h_r.at[o, d - 1], on_z(d)
            )

    for o in (0, 1, 3, 2):
        if o == 0:
            for h in range(2):
                relay(h, 1)
        for h in range(2):
            for way in range(2):
                if o >= 2 or way != o:
                    b_copies[h, way, o].wait_recv()
            d_copies[h, o].wait_recv()
        unpack(o)
        scores(o)
        give_terms(o)
        if o == 3:
            back_z(0)
        if o == 2:
            back_z(1)
            back_z(3)

    f_copies = []

    def image_rows(k, base, keep):
        cols = slice(base + k * 256, base + (k + 1) * 256)
        for j in range(4):
            lanes = slice(j * 256, (j + 1) * 256)
            keep(k, lanes, dot(coeffs[:, cols], panel[:, lanes], TN))

    def keep_partner(k, lanes, grads):
        igs[k * 256 : (k + 1) * 256, lanes] = grads.astype(BF)

    def keep_mine(k, lanes, grads):
        rows = slice(k * 256, (k + 1) * 256)
        mine[rows, lanes] = (grads + igr[rows, lanes].astype(F32)).astype(BF)

    def my_rows(k):
        f_copies[k].wait_recv()
        image_rows(k, 0, keep_mine)
        rows = pl.ds(k * 256, 256)
        stores.append(load(mine.at[rows], out_images.at[rows], in_sem.at[k]))

    stores = []

    def over_z(o):
        total = summed[o, pl.ds(pl.multiple_of(z * 16, 16), 16)].astype(F32)
        for d in (1, 7, 2, 6, 3, 5, 4):
            h_copies[o, d].wait_recv()
            total = total + got2[o, d - 1].astype(F32)
        return total

    def back_first(o):
        done[o - 1] = over_z(o).astype(BF)
        g_copies[o] = send(
            done.at[o - 1], got1.at[o - 1], g_s.at[o - 1], g_r.at[o - 1], on_own_first(4 - o)
        )

    def partner_rows(k):
        image_rows(k, ROWS, keep_partner)
        rows = pl.ds(k * 256, 256)
        f_copies.append(send(igs.at[rows], igr.at[rows], f_s.at[k], f_r.at[k], partner))

    partner_rows(0)
    partner_rows(1)
    back_z(2)
    partner_rows(2)
    partner_rows(3)
    my_rows(0)
    back_first(1)
    my_rows(1)
    back_first(3)
    my_rows(2)
    my_rows(3)
    back_first(2)
    total = over_z(0)
    for o in (1, 3, 2):
        g_copies[o].wait_recv()
        total = total + got1[o - 1].astype(F32)
    texts_in[:, :HALF] = total[:8]
    texts_in[:, HALF:] = total[8:]
    stores.append(load(texts_in, out_texts, row_sem.at[0]))

    for copy in sends:
        copy.wait_send()
    for copy in stores:
        copy.wait()


def finish(grads, text_grads, out_images, out_texts, low, full, text_low, text_full, in_sem, out_sem):
    loads, stores = [], []
    pieces = [pl.ds(k * 128, 128) for k in range(8)]
    for k, rows in enumerate(pieces):
        loads.append(pltpu.make_async_copy(grads.at[rows], low.at[rows], in_sem.at[k]))
    loads.append(pltpu.make_async_copy(text_grads, text_low, in_sem.at[8]))
    for copy in loads:
        copy.start()
    for k, rows in enumerate(pieces):
        loads[k].wait()
        full[rows] = low[rows].astype(F32) * logit_scale
        stores.append(pltpu.make_async_copy(full.at[rows], out_images.at[rows], out_sem.at[k]))
        stores[k].start()
    loads[8].wait()
    text_full[...] = text_low[...] * logit_scale
    stores.append(pltpu.make_async_copy(text_full, out_texts, out_sem.at[8]))
    stores[8].start()
    for copy in stores:
        copy.wait()


def shards(images, texts, row_lse, row_weights, pair_ids):
    hbm = pl.BlockSpec(memory_space=pltpu.HBM)
    dma = pltpu.SemaphoreType.DMA
    grads, text_grads = pl.pallas_call(
        kernel,
        out_shape=(
            jax.ShapeDtypeStruct((ROWS, D), BF),
            jax.ShapeDtypeStruct((8, D), F32),
        ),
        in_specs=[hbm] * 5,
        out_specs=(hbm, hbm),
        scratch_shapes=[
            pltpu.VMEM((ROWS, D), F32),
            pltpu.VMEM((8, D), F32),
            pltpu.VMEM((2, ROWS), F32),
            pltpu.VMEM((1, ROWS), jnp.int32),
            pltpu.VMEM((2 * ROWS, D), BF),
            pltpu.VMEM((2, 8, ROWS), F32),
            pltpu.VMEM((2, 4, 4, 64, HALF), BF),
            pltpu.VMEM((TEXTS, D), BF),
            pltpu.VMEM((TEXTS, 2 * ROWS), BF),
            pltpu.VMEM((4, 512, HALF), BF),
            pltpu.VMEM((4, 2, 3, 64, HALF), BF),
            pltpu.VMEM((4, 128, HALF), BF),
            pltpu.VMEM((3, 16, HALF), BF),
            pltpu.VMEM((3, 16, HALF), BF),
            pltpu.VMEM((4, 7, 16, HALF), BF),
            pltpu.VMEM((ROWS, D), BF),
            pltpu.VMEM((ROWS, D), BF),
            pltpu.VMEM((ROWS, D), BF),
            dma((4,)), dma((4,)), dma((4,)), dma((4,)), dma, dma, dma((7,)), dma((7,)),
            dma((2, 4)), dma((2, 4)), dma((2, 2, 4)), dma((2, 2, 4)), dma((2, 4)), dma((2, 4)),
            dma((4, 2, 3)), dma((4, 2, 3)), dma((4,)), dma((4,)), dma((3,)), dma((3,)), dma((4, 7)), dma((4, 7)),
        ],
        compiler_params=pltpu.CompilerParams(
            collective_id=0, has_side_effects=True, vmem_limit_bytes=62 * 10**6
        ),
        cost_estimate=pl.CostEstimate(flops=6 * ROWS * 2 * TEXTS * D, bytes_accessed=8 * ROWS * D, transcendentals=2 * ROWS * TEXTS),
        name="tile",
    )(
        images, texts, row_lse.reshape(1, ROWS), row_weights.reshape(1, ROWS), pair_ids.reshape(1, ROWS)
    )
    return pl.pallas_call(
        finish,
        out_shape=(
            jax.ShapeDtypeStruct((ROWS, D), F32),
            jax.ShapeDtypeStruct((8, D), F32),
        ),
        in_specs=[hbm] * 2,
        out_specs=(hbm, hbm),
        scratch_shapes=[
            pltpu.VMEM((ROWS, D), BF),
            pltpu.VMEM((ROWS, D), F32),
            pltpu.VMEM((8, D), F32),
            pltpu.VMEM((8, D), F32),
            dma((9,)),
            dma((9,)),
        ],
        compiler_params=pltpu.CompilerParams(vmem_limit_bytes=62 * 10**6),
        name="finish",
    )(grads, text_grads)


def solution(mesh):
    placed = (
        P(("blk", "group"), None),
        P(("blk", "group"), None),
        P(("blk", "group")),
        P(("blk", "group")),
        P(("blk", "group")),
    )
    return jax.shard_map(
        shards,
        mesh=mesh,
        in_specs=placed,
        out_specs=(P(("blk", "group"), None), P(("blk", "group"), None)),
        check_vma=False,
    )
```

```python
import math

import jax
import jax.numpy as jnp
from jax import lax
from jax.experimental import pallas as pl
from jax.experimental.pallas import tpu as pltpu
from jax.sharding import PartitionSpec as P

logit_scale = 100.0
log2e = math.log2(math.e)

MESH = pl.DeviceIdType.MESH
BF, F32 = jnp.bfloat16, jnp.float32
NN = (((1,), (0,)), ((), ()))
NT = (((1,), (1,)), ((), ()))
TN = (((0,), (0,)), ((), ()))

NX, NY, NZ = 4, 4, 8
ROWS, D = 1024, 1024
TEXTS = 1024
GROUP = 256
HALF = D // 2


def device(x, y, z, c):
    return (z * 2 + x // 2, (x % 2) * 8 + y * 2 + c)


def dot(a, b, dims):
    return lax.dot_general(a, b, dims, preferred_element_type=F32)


def kernel(
    images, texts, lse, weights, ids, out_images, out_texts,
    stage, texts_in, rows_in, ids_in, held, vec, blobs, panel, coeffs, sent, got, summed, done, got1, got2, mine, igs, igr,
    in_sem, row_sem, core_s, core_r, vec_s, vec_r, z_s, z_r, a_s, a_r, b_s, b_r, d_s, d_r,
    e_s, e_r, f_s, f_r, g_s, g_r, h_s, h_r,
):
    blk, group = lax.axis_index("blk"), lax.axis_index("group")
    z, x = blk // 2, (blk % 2) * 2 + group // 8
    y, c = (group // 2) % 4, group % 2
    zh = z // 4
    last, first = (x, y), (y, x)

    def on_last(h, o):
        return device((x + o) % NX, y, z, c) if h == 0 else device(x, (y + o) % NY, z, c)

    def on_first(h, o):
        return on_last(1 - h, o)

    def on_own_first(o):
        return device((x + o * zh) % NX, (y + o * (1 - zh)) % NY, z, c)

    def on_z(o):
        return device(x, y, (z + o) % NZ, c)

    partner = device(x, y, z, 1 - c)

    def load(src, dst, sem):
        copy = pltpu.make_async_copy(src, dst, sem)
        copy.start()
        return copy

    texts_load = load(texts, texts_in, row_sem.at[0])
    barrier = pltpu.get_barrier_semaphore()
    peers = [partner] + [on_z(o) for o in range(1, NZ)]
    peers += [on_last(h, o) for h in range(2) for o in range(1, 4)]
    for peer in peers:
        pl.semaphore_signal(barrier, inc=1, device_id=peer, device_id_type=MESH)

    loads = []
    for k in range(4):
        rows = pl.ds(k * 256, 256)
        loads.append(load(images.at[rows], stage.at[rows], in_sem.at[k]))
    row_loads = [
        load(lse, rows_in.at[pl.ds(0, 1)], row_sem.at[1]),
        load(weights, rows_in.at[pl.ds(1, 1)], row_sem.at[2]),
        load(ids, ids_in, row_sem.at[3]),
    ]

    sends = []

    def send(src, dst, ss, rs, peer):
        copy = pltpu.make_async_remote_copy(
            src_ref=src, dst_ref=dst, send_sem=ss, recv_sem=rs, device_id=peer, device_id_type=MESH
        )
        copy.start()
        sends.append(copy)
        return copy

    za = x * (1 - zh) + y * zh
    zb = y * (1 - zh) + x * zh
    place = blobs.at[zh, za, zb, pl.ds(pl.multiple_of((z % 4) * 16, 16), 16)]
    texts_load.wait()
    t = texts_in[...]
    place[...] = jnp.concatenate([t[:, :HALF], t[:, HALF:]], axis=0).astype(BF)

    pl.semaphore_wait(barrier, len(peers))

    z_copies = [send(place, place, z_s.at[o - 1], z_r.at[o - 1], on_z(o)) for o in (1, 7, 2, 6, 3, 5, 4)]

    vec[0] = jnp.zeros((8, ROWS), F32)
    for copy in row_loads:
        copy.wait()
    w = rows_in[1:2]
    vec[0, 0:1] = (jnp.log(w) - rows_in[0:1]) * log2e
    vec[0, 1:2] = ids_in[...].astype(F32)
    vec[0, 2:3] = w
    vec_copy = send(vec.at[0], vec.at[1], vec_s, vec_r, partner)

    for k in range(4):
        rows = pl.ds(k * 256, 256)
        loads[k].wait()
        held[rows] = stage[rows].astype(BF)

    core_copies = []
    for k in range(4):
        rows, there = pl.ds(k * 256, 256), pl.ds(ROWS + k * 256, 256)
        core_copies.append(send(held.at[rows], held.at[there], core_s.at[k], core_r.at[k], partner))
    for copy in z_copies:
        copy.wait_recv()

    a_copies, b_copies, d_copies = {}, {}, {}

    def place_of(h, o):
        return (first[h] - o + 4) % 4

    def to_last(h, o):
        blob = blobs.at[h, last[h], place_of(h, o)]
        for way, step in ((0, 1), (1, 3)):
            b_copies[h, way, o] = send(blob, blob, b_s.at[h, way, o], b_r.at[h, way, o], on_last(h, step))
        if o >= 2:
            d_copies[h, o] = send(blob, blob, d_s.at[h, o], d_r.at[h, o], on_last(h, 2))

    def relay(h, o):
        b_copies[h, o, o].wait_recv()
        blob = blobs.at[h, (last[h] + (3 if o == 0 else 1)) % 4, place_of(h, o)]
        d_copies[h, o] = send(blob, blob, d_s.at[h, o], d_r.at[h, o], on_last(h, 1 if o == 0 else 3))

    for h in range(2):
        blob = blobs.at[h, last[h], first[h]]
        for o in (1, 3, 2):
            a_copies[h, o] = send(blob, blob, a_s.at[h, o], a_r.at[h, o], on_first(h, o))
    for h in range(2):
        to_last(h, 0)
    for o in (1, 3, 2):
        for h in range(2):
            a_copies[h, o].wait_recv()
            to_last(h, o)
        if o == 1:
            for h in range(2):
                relay(h, 0)

    def unpack(o):
        for h in range(2):
            blob = blobs[h, :, place_of(h, o)].reshape(GROUP, HALF).astype(F32).reshape(16, 2, 8, HALF)
            rows = pl.ds(o * GROUP + h * 128, 128)
            panel[rows, :HALF] = blob[:, 0].reshape(128, HALF).astype(BF)
            panel[rows, HALF:] = blob[:, 1].reshape(128, HALF).astype(BF)

    def scores(o):
        rows = pl.ds(o * GROUP, GROUP)
        r = lax.broadcasted_iota(jnp.int32, (GROUP, 1), 0)
        a = (r & 127) >> 5
        zz = ((r >> 7) << 2) + ((r & 31) >> 3)
        chip = jnp.where(r >= 128, place_of(1, o) * 64 + a * 16, place_of(0, o) * 16 + a * 64)
        number = (zz * 256 + chip + c * 8 + (r & 7)).astype(F32)

        for side in range(2):
            for k in range(4):
                lanes = slice(k * 256, (k + 1) * 256)
                cols = slice(side * ROWS + k * 256, side * ROWS + (k + 1) * 256)
                s = dot(panel[rows], held[cols], NT)
                e = jnp.exp2(s * (logit_scale * log2e) + vec[side, 0:1, lanes])
                e = e - jnp.where(number == vec[side, 1:2, lanes], vec[side, 2:3, lanes], 0.0)
                coeffs[rows, cols] = e.astype(BF)

    def terms(o):
        rows = pl.ds(o * GROUP, GROUP)
        for j in range(2):
            lo = dot(coeffs[rows], held[:, j * 256 : (j + 1) * 256], NN)
            hi = dot(coeffs[rows], held[:, HALF + j * 256 : HALF + (j + 1) * 256], NN)
            both = jnp.stack([lo.reshape(32, 8, 256), hi.reshape(32, 8, 256)], axis=1).reshape(512, 256)
            sent[o, :, j * 256 : (j + 1) * 256] = both.astype(BF)

    def block(h, s):
        return pl.ds(pl.multiple_of(h * 256 + ((last[h] + s) % 4) * 64, 64), 64)

    for copy in core_copies:
        copy.wait_recv()
    vec_copy.wait_recv()

    e_copies = {}

    def give_terms(o):
        terms(o)
        for s in (2, 1, 3):
            for h in range(2):
                e_copies[h, o, s] = send(
                    sent.at[o, block(h, s)], got.at[o, h, s - 1],
                    e_s.at[o, h, s - 1], e_r.at[o, h, s - 1], on_last(h, s),
                )

    def over_last(h, o):
        total = sent[o, block(h, 0)].astype(F32)
        for s in (1, 3, 2):
            e_copies[h, o, s].wait_recv()
            total = total + got[o, h, s - 1].astype(F32)
        return total

    h_copies, g_copies = {}, {}

    def back_z(o):
        for h in range(2):
            summed[o, pl.ds(h * 64, 64)] = over_last(h, o).astype(BF)
        for d in (1, 7, 2, 6, 3, 5, 4):
            rows = pl.ds(pl.multiple_of(((z + d) % NZ) * 16, 16), 16)
            h_copies[o, d] = send(
                summed.at[o, rows], got2.at[o, d - 1], h_s.at[o, d - 1], h_r.at[o, d - 1], on_z(d)
            )

    for o in (0, 1, 3, 2):
        if o == 0:
            for h in range(2):
                relay(h, 1)
        for h in range(2):
            for way in range(2):
                if o >= 2 or way != o:
                    b_copies[h, way, o].wait_recv()
            d_copies[h, o].wait_recv()
        unpack(o)
        scores(o)
        give_terms(o)
        if o == 3:
            back_z(0)
        if o == 2:
            back_z(1)
            back_z(3)

    f_copies = []

    def image_rows(k, base, keep):
        cols = slice(base + k * 256, base + (k + 1) * 256)
        for j in range(4):
            lanes = slice(j * 256, (j + 1) * 256)
            keep(k, lanes, dot(coeffs[:, cols], panel[:, lanes], TN))

    def keep_partner(k, lanes, grads):
        igs[k * 256 : (k + 1) * 256, lanes] = grads.astype(BF)

    def keep_mine(k, lanes, grads):
        rows = slice(k * 256, (k + 1) * 256)
        mine[rows, lanes] = (grads + igr[rows, lanes].astype(F32)).astype(BF)

    def my_rows(k):
        f_copies[k].wait_recv()
        image_rows(k, 0, keep_mine)
        rows = pl.ds(k * 256, 256)
        stores.append(load(mine.at[rows], out_images.at[rows], in_sem.at[k]))

    stores = []

    def over_z(o):
        total = summed[o, pl.ds(pl.multiple_of(z * 16, 16), 16)].astype(F32)
        for d in (1, 7, 2, 6, 3, 5, 4):
            h_copies[o, d].wait_recv()
            total = total + got2[o, d - 1].astype(F32)
        return total

    def back_first(o):
        done[o - 1] = over_z(o).astype(BF)
        g_copies[o] = send(
            done.at[o - 1], got1.at[o - 1], g_s.at[o - 1], g_r.at[o - 1], on_own_first(4 - o)
        )

    def partner_rows(k):
        image_rows(k, ROWS, keep_partner)
        rows = pl.ds(k * 256, 256)
        f_copies.append(send(igs.at[rows], igr.at[rows], f_s.at[k], f_r.at[k], partner))

    partner_rows(0)
    partner_rows(1)
    back_z(2)
    partner_rows(2)
    partner_rows(3)
    my_rows(0)
    back_first(1)
    my_rows(1)
    back_first(3)
    my_rows(2)
    my_rows(3)
    back_first(2)
    total = over_z(0)
    for o in (1, 3, 2):
        g_copies[o].wait_recv()
        total = total + got1[o - 1].astype(F32)
    texts_in[:, :HALF] = total[:8]
    texts_in[:, HALF:] = total[8:]
    stores.append(load(texts_in, out_texts, row_sem.at[0]))

    for copy in sends:
        copy.wait_send()
    for copy in stores:
        copy.wait()


def finish(grads, text_grads, out_images, out_texts, low, full, text_low, text_full, in_sem, out_sem):
    loads, stores = [], []
    pieces = [pl.ds(k * 128, 128) for k in range(8)]
    for k, rows in enumerate(pieces):
        loads.append(pltpu.make_async_copy(grads.at[rows], low.at[rows], in_sem.at[k]))
    loads.append(pltpu.make_async_copy(text_grads, text_low, in_sem.at[8]))
    for copy in loads:
        copy.start()
    for k, rows in enumerate(pieces):
        loads[k].wait()
        full[rows] = low[rows].astype(F32) * logit_scale
        stores.append(pltpu.make_async_copy(full.at[rows], out_images.at[rows], out_sem.at[k]))
        stores[k].start()
    loads[8].wait()
    text_full[...] = text_low[...] * logit_scale
    stores.append(pltpu.make_async_copy(text_full, out_texts, out_sem.at[8]))
    stores[8].start()
    for copy in stores:
        copy.wait()


def shards(images, texts, row_lse, row_weights, pair_ids):
    hbm = pl.BlockSpec(memory_space=pltpu.HBM)
    dma = pltpu.SemaphoreType.DMA
    grads, text_grads = pl.pallas_call(
        kernel,
        out_shape=(
            jax.ShapeDtypeStruct((ROWS, D), BF),
            jax.ShapeDtypeStruct((8, D), F32),
        ),
        in_specs=[hbm] * 5,
        out_specs=(hbm, hbm),
        scratch_shapes=[
            pltpu.VMEM((ROWS, D), F32),
            pltpu.VMEM((8, D), F32),
            pltpu.VMEM((2, ROWS), F32),
            pltpu.VMEM((1, ROWS), jnp.int32),
            pltpu.VMEM((2 * ROWS, D), BF),
            pltpu.VMEM((2, 8, ROWS), F32),
            pltpu.VMEM((2, 4, 4, 64, HALF), BF),
            pltpu.VMEM((TEXTS, D), BF),
            pltpu.VMEM((TEXTS, 2 * ROWS), BF),
            pltpu.VMEM((4, 512, HALF), BF),
            pltpu.VMEM((4, 2, 3, 64, HALF), BF),
            pltpu.VMEM((4, 128, HALF), BF),
            pltpu.VMEM((3, 16, HALF), BF),
            pltpu.VMEM((3, 16, HALF), BF),
            pltpu.VMEM((4, 7, 16, HALF), BF),
            pltpu.VMEM((ROWS, D), BF),
            pltpu.VMEM((ROWS, D), BF),
            pltpu.VMEM((ROWS, D), BF),
            dma((4,)), dma((4,)), dma((4,)), dma((4,)), dma, dma, dma((7,)), dma((7,)),
            dma((2, 4)), dma((2, 4)), dma((2, 2, 4)), dma((2, 2, 4)), dma((2, 4)), dma((2, 4)),
            dma((4, 2, 3)), dma((4, 2, 3)), dma((4,)), dma((4,)), dma((3,)), dma((3,)), dma((4, 7)), dma((4, 7)),
        ],
        compiler_params=pltpu.CompilerParams(
            collective_id=0, has_side_effects=True, vmem_limit_bytes=62 * 10**6
        ),
        cost_estimate=pl.CostEstimate(flops=6 * ROWS * 2 * TEXTS * D, bytes_accessed=8 * ROWS * D, transcendentals=2 * ROWS * TEXTS),
        name="tile",
    )(
        images, texts, row_lse.reshape(1, ROWS), row_weights.reshape(1, ROWS), pair_ids.reshape(1, ROWS)
    )
    return pl.pallas_call(
        finish,
        out_shape=(
            jax.ShapeDtypeStruct((ROWS, D), F32),
            jax.ShapeDtypeStruct((8, D), F32),
        ),
        in_specs=[hbm] * 2,
        out_specs=(hbm, hbm),
        scratch_shapes=[
            pltpu.VMEM((ROWS, D), BF),
            pltpu.VMEM((ROWS, D), F32),
            pltpu.VMEM((8, D), F32),
            pltpu.VMEM((8, D), F32),
            dma((9,)),
            dma((9,)),
        ],
        compiler_params=pltpu.CompilerParams(vmem_limit_bytes=62 * 10**6),
        name="finish",
    )(grads, text_grads)


def solution(mesh):
    placed = (
        P(("blk", "group"), None),
        P(("blk", "group"), None),
        P(("blk", "group")),
        P(("blk", "group")),
        P(("blk", "group")),
    )
    return jax.shard_map(
        shards,
        mesh=mesh,
        in_specs=placed,
        out_specs=(P(("blk", "group"), None), P(("blk", "group"), None)),
        check_vma=False,
    )
```
